32 devices in a mesh: seq: 16 (over z, y, core), mp: 2 (over x).
Axes of the slice: x: 2, y: 2, z: 4, core: 2. Of those that a mesh axis runs over, the one named last changes fastest.
Arguments:
- normed: bfloat16 [8192, 2048], P('seq', 'mp'), may hold values from -18 to 18
- router: bfloat16 [2048], replicated, may hold values from -0.125 to 0.125
- light_qkv: bfloat16 [3, 2048, 1024], P(None, None, 'mp'), may hold values from -0.125 to 0.125
- light_out: bfloat16 [1024, 2048], P('mp'), may hold values from -0.1875 to 0.1875
- heavy_qkv: bfloat16 [3, 2048, 1024], P(None, 'seq', 'mp'), may hold values from -0.125 to 0.125
- heavy_out: bfloat16 [1024, 2048], P('mp', 'seq'), may hold values from -0.1875 to 0.1875
- query_slots: int32 [16, 32], P('seq'), may hold values from 0 to 511, as said below
- query_count: int32 [16], P('seq'), may hold values from 1 to 32, 256 in all
- key_slots: int32 [16, 32], P('seq'), may hold values from 0 to 511, as said below
- key_count: int32 [16], P('seq'), may hold values from 1 to 32, 256 in all
Outputs:
- mixed: bfloat16 [8192, 2048], P('seq', 'mp')
The draws below stay inside these ranges and needn't reach their ends.
Inputs may be any that keep to these rules, and one draw needn't show every extreme that they name: `query_slots`: each row holds 32 distinct positions of one shard's 512 tokens; only the first query_count entries of a row are live. `key_slots`: each row holds 32 distinct positions of one shard's 512 tokens; only the first key_count entries of a row are live. `query_count`: the counts sum to 256 and the largest is exactly 32. `key_count`: the counts sum to 256 and the largest is exactly 32.
All inputs are finite; a program needn't handle non-finite values.
Results may differ from the reference program's by a relative error of at most 0.012.
Values may be sent and summed in bfloat16 or wider, within the bound.
A program may use at most 128 MiB of HBM per device.

```python
import math
import jax
import jax.numpy as jnp
import numpy as np
from jax import lax

D = 2048
LHEADS = 16
HHEADS = 16
HEAD_DIM = 64
RADIUS = 64
TOK_DEV = 512
CAP = 32
SHARDS = 16
TOKENS = 8192


def draw_normed(key, part):
    base = jax.random.fold_in(jax.random.fold_in(key, 5), 0)
    values = jax.random.normal(base, (TOKENS, D), jnp.float32) * 1.75
    return jnp.clip(values, -7.0, 7.0).astype(jnp.bfloat16)


def slots_from(key, salt):
    shard_keys = jax.random.split(jax.random.fold_in(key, salt), SHARDS)

    def one_shard(shard_key):
        return jax.random.permutation(shard_key, TOK_DEV)[:CAP].astype(jnp.int32)
    return jax.vmap(one_shard)(shard_keys)


def draw_query_slots(key, part):
    return slots_from(key, 11)


def draw_key_slots(key, part):
    return slots_from(key, 23)


def block_scale(rng, extent, cuts, smallest, top_value):
    def one(position, blocks):
        heights = jax.random.uniform(jax.random.fold_in(jax.random.fold_in(rng, 6), position), (blocks,), jnp.float32, smallest / len(cuts), top_value / len(cuts))
        return jnp.repeat(jnp.exp(heights), extent[position] // blocks).reshape((-1,) + (1,) * (len(extent) - position - 1))

    gain = one(*cuts[0])
    for cut in cuts[1:]:
        gain = gain * one(*cut)
    return gain


def split_up(count, total, most, lean):
    weights = [(1 << 20) // math.isqrt(rank ** lean) + 1 for rank in range(2, count + 1)]
    spare, holding = total - most - (count - 1), [1] * (count - 1)
    while spare > 0:
        free = [i for i in range(count - 1) if holding[i] < most]
        mass, remaining = sum([weights[i] for i in free]), spare
        for i in free:
            more = min(most - holding[i], max(1, remaining * weights[i] // mass), spare)
            holding[i] = holding[i] + more
            spare = spare - more
    return np.array([most] + holding)


def uneven_parts(rng, count, total, bound, slope):
    if count == 2:
        one = jax.random.randint(rng, (), max(1, total - bound), min(bound, total - 1) + 1)
        return jnp.stack([one, total - one])
    lengths = jnp.asarray(split_up(count, total, bound, slope), jnp.int32)
    pairs = (count - 1) // 2
    donor, taker = lengths[1:1 + 2 * pairs:2], lengths[2:2 + 2 * pairs:2]
    room = jnp.minimum(donor - 1, bound - taker)
    moved = jax.random.randint(jax.random.fold_in(rng, 1), (pairs,), 0, 1 << 20) % (room + 1)
    lengths = lengths.at[1:1 + 2 * pairs:2].set(donor - moved).at[2:2 + 2 * pairs:2].set(taker + moved)
    return lengths[jax.random.permutation(jax.random.fold_in(rng, 2), count)]


def bell_draw(rng, dims, deviation, limit, shards=(), held_as=jnp.bfloat16):
    drawn = jax.random.normal(rng, dims, jnp.float32) * deviation
    if len(shards) > 0:
        drawn = block_scale(rng, dims, shards, -0.22, 0.18) * drawn
    return jnp.clip(drawn, min=-limit, max=limit).astype(held_as)


def setup_inputs(seed: int = 0) -> dict:
    keys = jax.random.split(jax.random.key(seed), 11)
    return {
        "normed": draw_normed(jax.random.fold_in(keys[10], 71), 0),
        "router": bell_draw(keys[1], (D,), D ** -0.5, 0.125),
        "light_qkv": bell_draw(keys[2], (3, D, LHEADS * HEAD_DIM), D ** -0.5, 0.125, ((2, 2),)),
        "light_out": bell_draw(keys[3], (LHEADS * HEAD_DIM, D), (LHEADS * HEAD_DIM) ** -0.5, 0.1875, ((0, 2),)),
        "heavy_qkv": bell_draw(keys[4], (3, D, HHEADS * HEAD_DIM), D ** -0.5, 0.125, ((1, 16), (2, 2))),
        "heavy_out": bell_draw(keys[5], (HHEADS * HEAD_DIM, D), (HHEADS * HEAD_DIM) ** -0.5, 0.1875, ((0, 2), (1, 16))),
        "query_slots": draw_query_slots(jax.random.fold_in(keys[10], 71), 0),
        "query_count": uneven_parts(keys[7], SHARDS, SHARDS * CAP // 2, CAP, 2).astype(jnp.int32),
        "key_slots": draw_key_slots(jax.random.fold_in(keys[10], 71), 0),
        "key_count": uneven_parts(keys[9], SHARDS, SHARDS * CAP // 2, CAP, 2).astype(jnp.int32),
    }


NEG = -1.0e30


def mix_heads(queries, key_rows, value_rows, allowed):
    length = queries.shape[0]
    head_count = queries.shape[1] // HEAD_DIM
    query_heads = queries.astype(jnp.float32).reshape(length, head_count, HEAD_DIM)
    key_heads = key_rows.astype(jnp.float32).reshape(key_rows.shape[0], head_count, HEAD_DIM)
    value_heads = value_rows.astype(jnp.float32).reshape(value_rows.shape[0], head_count, HEAD_DIM)
    scores = jnp.einsum("qhe,khe->hqk", query_heads, key_heads) * (HEAD_DIM ** -0.5)
    scores = jnp.where(allowed[None], scores, NEG)
    row_peak = jnp.max(scores, axis=2, keepdims=True)
    weights = jnp.where(allowed[None], jnp.exp(scores - row_peak), 0.0)
    row_total = jnp.sum(weights, axis=2)
    rounded = weights.astype(jnp.bfloat16).astype(jnp.float32)
    blended = jnp.einsum("hqk,khe->qhe", rounded, value_heads) / jnp.transpose(row_total)[:, :, None]
    return blended.reshape(length, head_count * HEAD_DIM).astype(jnp.bfloat16)


def reference(normed, router, light_qkv, light_out, heavy_qkv, heavy_out, query_slots, query_count, key_slots, key_count):
    block_rows = min(512, TOK_DEV)
    light_q = jnp.dot(normed, light_qkv[0], preferred_element_type=jnp.float32).astype(jnp.bfloat16)
    light_k = jnp.dot(normed, light_qkv[1], preferred_element_type=jnp.float32).astype(jnp.bfloat16)
    light_v = jnp.dot(normed, light_qkv[2], preferred_element_type=jnp.float32).astype(jnp.bfloat16)
    padding = jnp.zeros((RADIUS, light_k.shape[1]), jnp.bfloat16)
    keys_padded = jnp.concatenate([padding, light_k, padding], 0)
    values_padded = jnp.concatenate([padding, light_v, padding], 0)

    def light_block(offset):
        queries = lax.dynamic_slice_in_dim(light_q, offset, block_rows, 0)
        key_rows = lax.dynamic_slice_in_dim(keys_padded, offset, block_rows + 2 * RADIUS, 0)
        value_rows = lax.dynamic_slice_in_dim(values_padded, offset, block_rows + 2 * RADIUS, 0)
        query_pos = offset + jnp.arange(block_rows, dtype=jnp.int32)
        key_pos = offset - RADIUS + jnp.arange(block_rows + 2 * RADIUS, dtype=jnp.int32)
        distance = jnp.abs(query_pos[:, None] - key_pos[None, :])
        allowed = (distance <= RADIUS) & (key_pos[None, :] >= 0) & (key_pos[None, :] < TOKENS)
        return mix_heads(queries, key_rows, value_rows, allowed)

    offsets = jnp.arange(TOKENS // block_rows, dtype=jnp.int32) * block_rows
    context = lax.map(light_block, offsets).reshape(TOKENS, light_q.shape[1])

    shard_base = (jnp.arange(SHARDS, dtype=jnp.int32) * TOK_DEV)[:, None]
    slot_range = jnp.arange(CAP, dtype=jnp.int32)[None, :]
    query_rows = (query_slots + shard_base).reshape(-1)
    key_token_rows = (key_slots + shard_base).reshape(-1)
    query_live = (slot_range < query_count[:, None]).reshape(-1)
    key_live = (slot_range < key_count[:, None]).reshape(-1)
    query_inputs = normed[query_rows]
    key_inputs = normed[key_token_rows]
    heavy_q = jnp.dot(query_inputs, heavy_qkv[0], preferred_element_type=jnp.float32).astype(jnp.bfloat16)
    heavy_k = jnp.dot(key_inputs, heavy_qkv[1], preferred_element_type=jnp.float32).astype(jnp.bfloat16)
    heavy_v = jnp.dot(key_inputs, heavy_qkv[2], preferred_element_type=jnp.float32).astype(jnp.bfloat16)
    slot_total = SHARDS * CAP
    heavy_block = min(512, slot_total)
    allowed_keys = key_live[None, :]

    def heavy_part(offset):
        queries = lax.dynamic_slice_in_dim(heavy_q, offset, heavy_block, 0)
        return mix_heads(queries, heavy_k, heavy_v, allowed_keys)

    heavy_offsets = jnp.arange(slot_total // heavy_block, dtype=jnp.int32) * heavy_block
    heavy_context = lax.map(heavy_part, heavy_offsets).reshape(slot_total, heavy_q.shape[1])
    gate = jax.nn.sigmoid(jnp.dot(query_inputs, router, preferred_element_type=jnp.float32))
    gate = jnp.where(query_live, gate, 0.0)
    heavy_rows = jnp.dot(heavy_context, heavy_out, preferred_element_type=jnp.float32) * gate[:, None]
    combined = jnp.dot(context, light_out, preferred_element_type=jnp.float32)
    combined = combined.at[query_rows].add(heavy_rows)
    return combined.astype(jnp.bfloat16)
```

```python
import jax
import jax.numpy as jnp
from jax import lax
from jax.sharding import PartitionSpec as P

HEAD_DIM = 64
RADIUS = 64


NEG = -1e30


def padded(cells, sides, width):
    for axis, dim in sides:
        count = lax.axis_size(axis)
        ends = count - 1
        head = lax.slice_in_dim(cells, 0, width, axis=dim)
        tail = lax.slice_in_dim(cells, cells.shape[dim] - width, cells.shape[dim], axis=dim)
        cells = jnp.concatenate(
            [
                lax.ppermute(tail, axis, [(i, (i + 1) % count) for i in range(ends)]),
                cells,
                lax.ppermute(head, axis, [((i + 1) % count, i) for i in range(ends)]),
            ],
            axis=dim,
        )
    return cells


def mix_heads(queries, key_rows, value_rows, allowed):
    length = queries.shape[0]
    head_count = queries.shape[1] // HEAD_DIM
    query_heads = queries.reshape(length, head_count, HEAD_DIM)
    key_heads = key_rows.reshape(key_rows.shape[0], head_count, HEAD_DIM)
    value_heads = value_rows.reshape(value_rows.shape[0], head_count, HEAD_DIM)
    scores = jnp.einsum(
        "qhe,khe->hqk", query_heads, key_heads, preferred_element_type=jnp.float32
    ) * HEAD_DIM ** (-0.5)
    scores = jnp.where(allowed[None], scores, NEG)
    row_peak = jnp.max(scores, axis=2, keepdims=True)
    weights = jnp.where(allowed[None], jnp.exp(scores - row_peak), 0.0)
    row_total = jnp.sum(weights, axis=2)
    blended = jnp.einsum(
        "hqk,khe->qhe",
        weights.astype(jnp.bfloat16),
        value_heads,
        preferred_element_type=jnp.float32,
    )
    blended = blended / jnp.transpose(row_total)[:, :, None]
    return blended.reshape(length, head_count * HEAD_DIM).astype(jnp.bfloat16)


def shards(
    normed,
    router,
    light_qkv,
    light_out,
    heavy_qkv,
    heavy_out,
    query_slots,
    query_count,
    key_slots,
    key_count,
):
    local_rows = normed.shape[0]
    shard_index = lax.axis_index("seq")
    shard_total = lax.axis_size("seq")
    capacity = query_slots.shape[1]
    width = normed.shape[1]
    me = lax.axis_index("mp")
    swap = [(0, 1), (1, 0)]
    other = lax.ppermute(normed, "mp", swap)
    qkv_mine = lax.dynamic_slice_in_dim(light_qkv, me * width, width, axis=1)
    qkv_other = lax.dynamic_slice_in_dim(light_qkv, (1 - me) * width, width, axis=1)
    product = jnp.einsum("td,cdh->cth", normed, qkv_mine, preferred_element_type=jnp.float32)
    product = product + jnp.einsum(
        "td,cdh->cth", other, qkv_other, preferred_element_type=jnp.float32
    )
    product = product.astype(jnp.bfloat16)
    queries = product[0]
    paired = product[1:]
    paired = padded(paired, (("seq", 1),), RADIUS)
    key_rows = paired[0]
    value_rows = paired[1]
    block_rows = min(512, local_rows)
    first_row = shard_index * local_rows
    query_pos = first_row + 0 + jnp.arange(block_rows, dtype=jnp.int32)
    key_pos = first_row + 0 - RADIUS + jnp.arange(block_rows + 2 * RADIUS, dtype=jnp.int32)
    distance = jnp.abs(query_pos[:, None] - key_pos[None, :])
    allowed = (
        (distance <= RADIUS)
        & (key_pos[None, :] >= 0)
        & (key_pos[None, :] < local_rows * shard_total)
    )
    outputs = mix_heads(queries, key_rows, value_rows, allowed)
    out_mine = lax.dynamic_slice_in_dim(light_out, me * width, width, axis=1)
    out_other = lax.dynamic_slice_in_dim(light_out, (1 - me) * width, width, axis=1)
    away = jnp.dot(outputs, out_other, preferred_element_type=jnp.float32).astype(jnp.bfloat16)
    arrived = lax.ppermute(away, "mp", swap)
    home = jnp.dot(outputs, out_mine, preferred_element_type=jnp.float32)
    slot_range = jnp.arange(capacity, dtype=jnp.int32)
    query_live = slot_range < query_count[0]
    key_live = (slot_range < key_count[0]).astype(jnp.bfloat16)
    def rows_of(slots):
        here, there = normed[slots], other[slots]
        first = jnp.where(me == 0, here, there)
        second = jnp.where(me == 0, there, here)
        return jnp.concatenate([first, second], axis=1)

    query_inputs = rows_of(query_slots[0])
    key_inputs = rows_of(key_slots[0])
    portion = lax.all_gather(heavy_qkv, "seq", axis=1, tiled=True)
    heavy_query = jnp.dot(query_inputs, portion[0], preferred_element_type=jnp.float32)
    heavy_key = jnp.dot(key_inputs, portion[1], preferred_element_type=jnp.float32)
    heavy_value = jnp.dot(key_inputs, portion[2], preferred_element_type=jnp.float32)
    heavy_query = heavy_query.astype(jnp.bfloat16)
    heavy_key = heavy_key.astype(jnp.bfloat16)
    heavy_value = heavy_value.astype(jnp.bfloat16)
    head_count = heavy_query.shape[1] // HEAD_DIM
    scale = HEAD_DIM ** (-0.5)
    query_heads = heavy_query.reshape(capacity, head_count, HEAD_DIM)
    row_peak = jnp.full((capacity, head_count), NEG, jnp.float32)
    size = heavy_key.shape[1]
    marks = jnp.broadcast_to(key_live[:, None], (capacity, 128))
    packed = jnp.concatenate([heavy_key, heavy_value, marks], axis=1)
    packed = lax.all_gather(packed, "seq", axis=0, tiled=True)
    key_part = packed[:, :size]
    value_part = packed[:, size : 2 * size]
    live_part = packed[:, 2 * size]
    length = key_part.shape[0]
    key_heads = key_part.reshape(length, head_count, HEAD_DIM)
    value_heads = value_part.reshape(length, head_count, HEAD_DIM)
    live = live_part[None, None, :] > 0
    scores = (
        jnp.einsum("qhe,khe->qhk", query_heads, key_heads, preferred_element_type=jnp.float32)
        * scale
    )
    scores = jnp.where(live, scores, NEG)
    new_peak = jnp.maximum(row_peak, jnp.max(scores, axis=2))
    weights = jnp.where(live, jnp.exp(scores - new_peak[:, :, None]), 0.0)
    row_total = jnp.sum(weights, axis=2)
    blended = jnp.einsum(
        "qhk,khe->qhe",
        weights.astype(jnp.bfloat16),
        value_heads,
        preferred_element_type=jnp.float32,
    )
    row_peak, row_total, blended = (new_peak, row_total, blended)
    blended = blended / row_total[:, :, None]
    heavy_context = blended.reshape(capacity, head_count * HEAD_DIM).astype(jnp.bfloat16)
    gate = jax.nn.sigmoid(jnp.dot(query_inputs, router, preferred_element_type=jnp.float32))
    gate = jnp.where(query_live, gate, 0.0)
    heavy_rows = (
        jnp.dot(
            heavy_context,
            lax.all_gather(heavy_out, "seq", axis=1, tiled=True),
            preferred_element_type=jnp.float32,
        )
        * gate[:, None]
    )
    rows_mine = lax.dynamic_slice_in_dim(heavy_rows, me * width, width, axis=1)
    rows_other = lax.dynamic_slice_in_dim(heavy_rows, (1 - me) * width, width, axis=1)
    rows_mine = rows_mine + lax.ppermute(rows_other, "mp", swap)
    combined = home + arrived.astype(jnp.float32)
    return combined.at[query_slots[0]].add(rows_mine).astype(jnp.bfloat16)


def solution(mesh):
    in_specs = (
        P("seq", "mp"),
        P(),
        P(None, None, "mp"),
        P("mp", None),
        P(None, "seq", "mp"),
        P("mp", "seq"),
        P("seq", None),
        P("seq"),
        P("seq", None),
        P("seq"),
    )
    out_specs = P("seq", "mp")
    return jax.shard_map(shards, mesh=mesh, in_specs=in_specs, out_specs=out_specs, check_vma=False)
```

```python
import functools

import jax
import jax.numpy as jnp
from jax import lax
from jax.experimental import pallas as pl
from jax.experimental.pallas import tpu as pltpu
from jax.sharding import PartitionSpec as P

HEAD_DIM = 64
RADIUS = 64
PAIR = 2 * HEAD_DIM
BLOCK = 128
NEG = -1e30
F32 = jnp.float32
BF16 = jnp.bfloat16
MESH = pl.DeviceIdType.MESH
NT = (((1,), (1,)), ((), ()))


def dot(a, b):
    return jnp.dot(a, b, preferred_element_type=F32)


def dot_nt(a, b):
    return lax.dot_general(a, b, NT, preferred_element_type=F32)


def attend(q, k, v, allowed, scale):
    rows = q.shape[0]
    low = lax.broadcasted_iota(jnp.int32, q.shape, 1) < HEAD_DIM
    zero = jnp.zeros_like(q)
    both = jnp.concatenate([jnp.where(low, q, zero), jnp.where(low, zero, q)], axis=0)
    scores = jnp.where(allowed, dot_nt(both, k) * scale, NEG)
    weights = jnp.exp(scores - jnp.max(scores, axis=1, keepdims=True))
    total = jnp.sum(weights, axis=1, keepdims=True)
    blended = dot(weights.astype(BF16), v) / total
    return jnp.where(low, blended[:rows], blended[rows:]).astype(BF16)


def kernel(
    count,
    normed,
    router,
    light_qkv,
    light_out,
    heavy,
    query_col,
    query_row,
    key_col,
    query_count,
    key_count,
    result,
    other,
    wide,
    narrow,
    pool,
    share,
    queries,
    window,
    context,
    away,
    arrived,
    inputs,
    heavy_kv,
    rows_away,
    rows_in,
    load_sem,
    recv_sem,
    up_sem,
    down_sem,
    cross_sem,
    core_sem,
    feat_send,
    feat_recv,
    halo_send,
    halo_recv,
    out_send,
    out_recv,
    row_send,
    row_recv,
):
    tokens, width = normed.shape
    size = narrow.shape[0]
    depth = heavy.shape[1]
    cap = key_col.shape[0]
    scale = HEAD_DIM ** (-0.5)
    me = lax.axis_index("seq")
    part = lax.axis_index("mp")
    peer = 1 - part
    levels = count // 4
    z = me // 4
    y = (me // 2) % 2
    c = me % 2
    left = lax.rem(me + count - 1, count)
    right = lax.rem(me + 1, count)
    top = z < levels - 1
    bottom = z > 0

    def slot(o, yy, cc):
        return (o * 2 + yy) * 2 + cc

    to_peer = {"mp": peer}
    to_up = {"seq": jnp.minimum(me + 4, count - 1)}
    to_down = {"seq": jnp.maximum(me - 4, 0)}
    to_cross = {"seq": slot(z, 1 - y, c)}
    to_core = {"seq": slot(z, y, 1 - c)}

    barrier = pltpu.get_barrier_semaphore()
    for dest in (to_peer, to_cross, to_core, {"seq": left}, {"seq": right}):
        pl.semaphore_signal(barrier, inc=1, device_id=dest, device_id_type=MESH)

    @pl.when(top)
    def _():
        pl.semaphore_signal(barrier, inc=1, device_id=to_up, device_id_type=MESH)

    @pl.when(bottom)
    def _():
        pl.semaphore_signal(barrier, inc=1, device_id=to_down, device_id_type=MESH)

    load_qkv = pltpu.make_async_copy(light_qkv, wide, load_sem.at[0])
    load_qkv.start()
    load_out = pltpu.make_async_copy(light_out, narrow, load_sem.at[1])
    load_out.start()
    pool[:, pl.ds(pl.multiple_of(me * depth, depth), depth), :] = heavy[...]

    pl.semaphore_wait(barrier, 5 + top.astype(jnp.int32) + bottom.astype(jnp.int32))

    def remote(src, dst, send, recv, dest):
        return pltpu.make_async_remote_copy(
            src_ref=src,
            dst_ref=dst,
            send_sem=send,
            recv_sem=recv,
            device_id=dest,
            device_id_type=MESH,
        )

    def view(chunk, s):
        if chunk < 2:
            rows = pl.ds(pl.multiple_of(s * depth, depth), depth)
            return pool.at[pl.ds(2 * chunk, 2), rows, :]
        return heavy_kv.at[pl.ds(pl.multiple_of(s * cap, cap), cap), :]

    def hop(chunk, s, send, dest):
        return remote(view(chunk, s), view(chunk, s), send, recv_sem.at[chunk, s], dest)

    def up(chunk, o):
        return hop(chunk, slot(o, y, c), up_sem.at[chunk, o], to_up)

    def down(chunk, o):
        return hop(chunk, slot(o, y, c), down_sem.at[chunk, o], to_down)

    def cross(chunk, o):
        return hop(chunk, slot(o, y, c), cross_sem.at[chunk, o], to_cross)

    def core(chunk, o, yy):
        return hop(chunk, slot(o, yy, c), core_sem.at[chunk, o * 2 + yy], to_core)

    def landed(chunk, s):
        hop(chunk, s, core_sem.at[chunk, 0], to_core).wait_recv()

    def own(chunk):
        @pl.when(top)
        def _():
            up(chunk, z).start()

        @pl.when(bottom)
        def _():
            down(chunk, z).start()

        cross(chunk, z).start()
        core(chunk, z, y).start()

    def along(chunk, d):
        @pl.when(z - d >= 0)
        def _():
            o = z - d
            landed(chunk, slot(o, y, c))

            @pl.when(top)
            def _():
                up(chunk, o).start()

            cross(chunk, o).start()
            core(chunk, o, y).start()

        @pl.when(z + d < levels)
        def _():
            o = z + d
            landed(chunk, slot(o, y, c))

            @pl.when(bottom)
            def _():
                down(chunk, o).start()

            cross(chunk, o).start()
            core(chunk, o, y).start()

    def across(chunk, d):
        @pl.when(z - d >= 0)
        def _():
            landed(chunk, slot(z - d, 1 - y, c))
            core(chunk, z - d, 1 - y).start()

        if d > 0:

            @pl.when(z + d < levels)
            def _():
                landed(chunk, slot(z + d, 1 - y, c))
                core(chunk, z + d, 1 - y).start()

    def events(chunk):
        for d in range(1, levels):
            yield functools.partial(along, chunk, d)
            yield functools.partial(across, chunk, d - 1)
        yield functools.partial(across, chunk, levels - 1)

    pending = [list(events(chunk)) for chunk in range(3)]

    def advance(chunk, steps=None):
        steps = len(pending[chunk]) if steps is None else min(steps, len(pending[chunk]))
        for _ in range(steps):
            pending[chunk].pop(0)()

    def gathered(chunk):
        for o in range(levels):
            for yy in range(2):
                landed(chunk, slot(o, yy, 1 - c))

    def drain(chunk):
        for o in range(levels):

            @pl.when(top & (z >= o))
            def _():
                up(chunk, o).wait_send()

            @pl.when(bottom & (z <= o))
            def _():
                down(chunk, o).wait_send()

            cross(chunk, o).wait_send()
            for yy in range(2):
                core(chunk, o, yy).wait_send()

    half = tokens // 2

    def feature(i):
        rows = pl.ds(i * half, half)
        return remote(normed.at[rows], other.at[rows], feat_send.at[i], feat_recv.at[i], to_peer)

    own(0)
    feature(0).start()
    feature(1).start()
    own(1)

    mine_rows = pl.ds(pl.multiple_of(part * width, width), width)
    peer_rows = pl.ds(pl.multiple_of(peer * width, width), width)

    query_hot = (
        lax.broadcasted_iota(jnp.int32, (cap, tokens), 1) == query_col[...]
    ).astype(BF16)
    key_hot = (lax.broadcasted_iota(jnp.int32, (cap, tokens), 1) == key_col[...]).astype(BF16)
    inputs[0, :, mine_rows] = dot(query_hot, normed[...]).astype(BF16)
    inputs[1, :, mine_rows] = dot(key_hot, normed[...]).astype(BF16)
    load_qkv.wait()
    for j in range(3):
        share[j] = dot(normed[...], wide[j, mine_rows, :])
    def project(i):
        feature(i).wait_recv()
        rows = pl.ds(i * half, half)
        for j in range(3):
            value = share[j, rows, :] + dot(other[rows, :], wide[j, peer_rows, :])
            if j == 0:
                queries[rows, :] = value.astype(BF16)
            else:
                window[pl.ds(RADIUS + i * half, half), pl.ds((j - 1) * size, size)] = value.astype(
                    BF16
                )

    advance(0, 2)
    project(0)
    advance(0, 3)
    project(1)

    edge = pl.ds(RADIUS, RADIUS)
    last = pl.ds(tokens, RADIUS)
    halos = [
        remote(
            window.at[edge],
            window.at[pl.ds(tokens + RADIUS, RADIUS)],
            halo_send.at[0],
            halo_recv.at[0],
            {"seq": left},
        ),
        remote(
            window.at[last],
            window.at[pl.ds(0, RADIUS)],
            halo_send.at[1],
            halo_recv.at[1],
            {"seq": right},
        ),
    ]
    for halo in halos:
        halo.start()

    inputs[0, :, peer_rows] = dot(query_hot, other[...]).astype(BF16)
    inputs[1, :, peer_rows] = dot(key_hot, other[...]).astype(BF16)
    advance(0)
    gathered(0)
    slots = pl.ds(pl.multiple_of(me * cap, cap), cap)
    heavy_kv[slots, pl.ds(0, size)] = dot(inputs[1], pool[0]).astype(BF16)
    heavy_kv[slots, pl.ds(size, size)] = dot(inputs[1], pool[1]).astype(BF16)
    heavy_kv[slots, pl.ds(2 * size, BLOCK)] = (
        lax.broadcasted_iota(jnp.int32, (cap, BLOCK), 0) < key_count[...]
    ).astype(BF16)
    own(2)
    advance(1, 2)
    load_out.wait()
    blocks = tokens // BLOCK

    def outgoing(r):
        rows = pl.ds(pl.multiple_of(r * BLOCK, BLOCK), BLOCK)
        return remote(away.at[rows], arrived.at[rows], out_send.at[r], out_recv.at[r], to_peer)

    def block(r):
        rows = pl.ds(pl.multiple_of(r * BLOCK, BLOCK), BLOCK)
        reach = pl.ds(pl.multiple_of(r * BLOCK, BLOCK), BLOCK + 2 * RADIUS)
        shape = (2 * BLOCK, BLOCK + 2 * RADIUS)
        row = lax.broadcasted_iota(jnp.int32, shape, 0)
        row = jnp.where(row < BLOCK, row, row - BLOCK)
        column = lax.broadcasted_iota(jnp.int32, shape, 1)
        gap = column - row
        place = me * tokens + r * BLOCK - RADIUS + column
        allowed = (gap >= 0) & (gap <= 2 * RADIUS) & (place >= 0) & (place < count * tokens)
        for h in range(size // PAIR):
            lanes = pl.ds(h * PAIR, PAIR)
            context[rows, lanes] = attend(
                queries[rows, lanes],
                window[reach, lanes],
                window[reach, pl.ds(size + h * PAIR, PAIR)],
                allowed,
                scale,
            )
        away[rows, :] = dot(context[rows, :], narrow[:, peer_rows]).astype(BF16)
        outgoing(r).start()

    def inner(r, carry):
        block(r)
        return carry

    lax.fori_loop(1, blocks - 1, inner, 0)
    advance(1, 2)
    for halo in halos:
        halo.wait_recv()

    def outer(e, carry):
        block(e * (blocks - 1))
        return carry

    lax.fori_loop(0, 2, outer, 0)
    advance(1)
    advance(2, 2)
    pieces = width // size
    for j in range(pieces):
        columns = pl.ds(pl.multiple_of(part * width + j * size, BLOCK), size)
        share[j] = dot(context[...], narrow[:, columns])
    advance(2)
    gathered(1)
    heavy_q = dot(inputs[0], pool[2]).astype(BF16)
    logit = jnp.sum(
        inputs[0].astype(F32) * router[...].astype(F32), axis=1, keepdims=True
    )
    gate = 1.0 / (1.0 + jnp.exp(-logit))
    live_slot = lax.broadcasted_iota(jnp.int32, (cap, 1), 0) < query_count[...]
    gate = jnp.where(live_slot, gate, 0.0)
    gathered(2)
    first = (lax.broadcasted_iota(jnp.int32, (2 * cap, BLOCK), 1) == 0).astype(BF16)
    live = dot_nt(first, heavy_kv[:, pl.ds(2 * size, BLOCK)]) > 0.5
    heavy_context = jnp.concatenate(
        [
            attend(
                heavy_q[:, h * PAIR : (h + 1) * PAIR],
                heavy_kv[:, pl.ds(h * PAIR, PAIR)],
                heavy_kv[:, pl.ds(size + h * PAIR, PAIR)],
                live,
                scale,
            )
            for h in range(size // PAIR)
        ],
        axis=1,
    )
    rows_away[...] = dot_nt(heavy_context, pool[3, peer_rows, :]) * gate
    row_copy = remote(rows_away, rows_in, row_send.at[0], row_recv.at[0], to_peer)
    row_copy.start()
    rows_mine = dot_nt(heavy_context, pool[3, mine_rows, :]) * gate
    place_hot = (
        lax.broadcasted_iota(jnp.int32, (tokens, cap), 0) == query_row[...]
    ).astype(BF16)
    row_copy.wait_recv()
    routed = (rows_mine + rows_in[...]).astype(BF16)
    for r in [*range(1, blocks - 1), 0, blocks - 1]:
        outgoing(r).wait_recv()
        rows = pl.ds(r * BLOCK, BLOCK)
        for j in range(pieces):
            columns = pl.ds(j * size, size)
            added = dot(place_hot[r * BLOCK : (r + 1) * BLOCK], routed[:, j * size : (j + 1) * size])
            result[rows, columns] = (
                share[j, rows, :] + arrived[rows, columns].astype(F32) + added
            ).astype(BF16)

    for chunk in range(3):
        drain(chunk)
    for i in range(2):
        feature(i).wait_send()
        halos[i].wait_send()
    for r in range(blocks):
        outgoing(r).wait_send()
    row_copy.wait_send()


def shards(
    count,
    normed,
    router,
    light_qkv,
    light_out,
    heavy_qkv,
    heavy_out,
    query_slots,
    query_count,
    key_slots,
    key_count,
):
    tokens, width = normed.shape
    size = light_out.shape[0]
    model = router.shape[0]
    cap = query_slots.shape[1]
    levels = count // 4
    heavy = jnp.concatenate(
        [heavy_qkv[1:], heavy_qkv[:1], jnp.transpose(heavy_out)[None]], axis=0
    )
    vmem = pl.BlockSpec(memory_space=pltpu.VMEM)
    anywhere = pl.BlockSpec(memory_space=pl.ANY)
    blocks = tokens // BLOCK
    dma = pltpu.SemaphoreType.DMA
    return pl.pallas_call(
        functools.partial(kernel, count),
        out_shape=jax.ShapeDtypeStruct((tokens, width), BF16),
        in_specs=[vmem, vmem, anywhere, anywhere] + [vmem] * 6,
        out_specs=vmem,
        scratch_shapes=[
            pltpu.VMEM((tokens, width), BF16),
            pltpu.VMEM(light_qkv.shape, BF16),
            pltpu.VMEM(light_out.shape, BF16),
            pltpu.VMEM((4, model, size), BF16),
            pltpu.VMEM((3, tokens, size), F32),
            pltpu.VMEM((tokens, size), BF16),
            pltpu.VMEM((tokens + 2 * RADIUS, 2 * size), BF16),
            pltpu.VMEM((tokens, size), BF16),
            pltpu.VMEM((tokens, width), BF16),
            pltpu.VMEM((tokens, width), BF16),
            pltpu.VMEM((2, cap, model), BF16),
            pltpu.VMEM((count * cap, 2 * size + BLOCK), BF16),
            pltpu.VMEM((cap, width), F32),
            pltpu.VMEM((cap, width), F32),
            dma((2,)),
            dma((3, count)),
            dma((3, levels)),
            dma((3, levels)),
            dma((3, levels)),
            dma((3, 2 * levels)),
            dma((2,)),
            dma((2,)),
            dma((2,)),
            dma((2,)),
            dma((blocks,)),
            dma((blocks,)),
            dma((1,)),
            dma((1,)),
        ],
        compiler_params=pltpu.CompilerParams(
            collective_id=0, has_side_effects=True, vmem_limit_bytes=52 * 1024 * 1024
        ),
    )(
        normed,
        router[None],
        light_qkv,
        light_out,
        heavy,
        jnp.reshape(query_slots, (cap, 1)),
        query_slots,
        jnp.reshape(key_slots, (cap, 1)),
        query_count[None],
        key_count[None],
    )


def solution(mesh):
    in_specs = (
        P("seq", "mp"),
        P(),
        P(None, None, "mp"),
        P("mp", None),
        P(None, "seq", "mp"),
        P("mp", "seq"),
        P("seq", None),
        P("seq"),
        P("seq", None),
        P("seq"),
    )
    return jax.shard_map(
        functools.partial(shards, mesh.shape["seq"]),
        mesh=mesh,
        in_specs=in_specs,
        out_specs=P("seq", "mp"),
        check_vma=False,
    )
```

```python
import functools

import jax
import jax.numpy as jnp
from jax import lax
from jax.experimental import pallas as pl
from jax.experimental.pallas import tpu as pltpu
from jax.sharding import PartitionSpec as P

HEAD_DIM = 64
RADIUS = 64
PAIR = 2 * HEAD_DIM
BLOCK = 128
NEG = -1e30
F32 = jnp.float32
BF16 = jnp.bfloat16
MESH = pl.DeviceIdType.MESH
NT = (((1,), (1,)), ((), ()))


def dot(a, b):
    return jnp.dot(a, b, preferred_element_type=F32)


def dot_nt(a, b):
    return lax.dot_general(a, b, NT, preferred_element_type=F32)


def dot_tn(a, b):
    return lax.dot_general(a, b, (((0,), (0,)), ((), ())), preferred_element_type=F32)


def attend(q, k, v, allowed, scale):
    rows = q.shape[0]
    low = lax.broadcasted_iota(jnp.int32, q.shape, 1) < HEAD_DIM
    zero = jnp.zeros_like(q)
    both = jnp.concatenate([jnp.where(low, q, zero), jnp.where(low, zero, q)], axis=0)
    scores = jnp.where(allowed, dot_nt(both, k) * scale, NEG)
    weights = jnp.exp(scores - jnp.max(scores, axis=1, keepdims=True))
    total = jnp.sum(weights, axis=1, keepdims=True)
    blended = dot(weights.astype(BF16), v) / total
    return jnp.where(low, blended[:rows], blended[rows:]).astype(BF16)


def kernel(
    count,
    normed,
    router,
    light_qkv,
    light_out,
    heavy_qkv,
    heavy_out,
    query_row,
    key_row,
    query_count,
    key_count,
    result,
    other,
    wide,
    narrow,
    pool,
    share,
    queries,
    window,
    context,
    away,
    arrived,
    inputs,
    heavy_kv,
    rows_away,
    rows_in,
    load_sem,
    recv_sem,
    up_sem,
    down_sem,
    cross_sem,
    core_sem,
    feat_send,
    feat_recv,
    halo_send,
    halo_recv,
    out_send,
    out_recv,
    row_send,
    row_recv,
):
    tokens, width = normed.shape
    size = narrow.shape[0]
    depth = heavy_qkv.shape[1]
    cap = key_row.shape[1]
    scale = HEAD_DIM ** (-0.5)
    me = lax.axis_index("seq")
    part = lax.axis_index("mp")
    peer = 1 - part
    levels = count // 4
    z = me // 4
    y = (me // 2) % 2
    c = me % 2
    left = lax.rem(me + count - 1, count)
    right = lax.rem(me + 1, count)
    top = z < levels - 1
    bottom = z > 0

    def slot(o, yy, cc):
        return (o * 2 + yy) * 2 + cc

    to_peer = {"mp": peer}
    to_up = {"seq": jnp.minimum(me + 4, count - 1)}
    to_down = {"seq": jnp.maximum(me - 4, 0)}
    to_cross = {"seq": slot(z, 1 - y, c)}
    to_core = {"seq": slot(z, y, 1 - c)}

    barrier = pltpu.get_barrier_semaphore()
    for dest in (to_peer, to_cross, to_core, {"seq": left}, {"seq": right}):
        pl.semaphore_signal(barrier, inc=1, device_id=dest, device_id_type=MESH)

    @pl.when(top)
    def _():
        pl.semaphore_signal(barrier, inc=1, device_id=to_up, device_id_type=MESH)

    @pl.when(bottom)
    def _():
        pl.semaphore_signal(barrier, inc=1, device_id=to_down, device_id_type=MESH)

    load_qkv = pltpu.make_async_copy(light_qkv, wide, load_sem.at[0])
    load_qkv.start()
    load_out = pltpu.make_async_copy(light_out, narrow, load_sem.at[1])
    load_out.start()
    held = pl.ds(pl.multiple_of(me * depth, depth), depth)
    for to, source in ((0, 1), (1, 2), (2, 0)):
        pool[to, held, :] = heavy_qkv[source]
    square = (depth, depth)
    unit = lax.broadcasted_iota(jnp.int32, square, 0) == lax.broadcasted_iota(jnp.int32, square, 1)
    pool[3, held, :] = dot_nt(unit.astype(BF16), heavy_out[...]).astype(BF16)

    pl.semaphore_wait(barrier, 5 + top.astype(jnp.int32) + bottom.astype(jnp.int32))

    def remote(src, dst, send, recv, dest):
        return pltpu.make_async_remote_copy(
            src_ref=src,
            dst_ref=dst,
            send_sem=send,
            recv_sem=recv,
            device_id=dest,
            device_id_type=MESH,
        )

    def view(chunk, s):
        if chunk != 2:
            rows = pl.ds(pl.multiple_of(s * depth, depth), depth)
            first, many = {0: (0, 2), 1: (2, 1), 3: (3, 1)}[chunk]
            return pool.at[pl.ds(first, many), rows, :]
        return heavy_kv.at[pl.ds(pl.multiple_of(s * cap, cap), cap), :]

    def hop(chunk, s, send, dest):
        return remote(view(chunk, s), view(chunk, s), send, recv_sem.at[chunk, s], dest)

    def up(chunk, o):
        return hop(chunk, slot(o, y, c), up_sem.at[chunk, o], to_up)

    def down(chunk, o):
        return hop(chunk, slot(o, y, c), down_sem.at[chunk, o], to_down)

    def cross(chunk, o):
        return hop(chunk, slot(o, y, c), cross_sem.at[chunk, o], to_cross)

    def core(chunk, o, yy):
        return hop(chunk, slot(o, yy, c), core_sem.at[chunk, o * 2 + yy], to_core)

    def landed(chunk, s):
        hop(chunk, s, core_sem.at[chunk, 0], to_core).wait_recv()

    def own(chunk):
        @pl.when(top)
        def _():
            up(chunk, z).start()

        @pl.when(bottom)
        def _():
            down(chunk, z).start()

        cross(chunk, z).start()
        core(chunk, z, y).start()

    def along(chunk, d):
        @pl.when(z - d >= 0)
        def _():
            o = z - d
            landed(chunk, slot(o, y, c))

            @pl.when(top)
            def _():
                up(chunk, o).start()

            cross(chunk, o).start()
            core(chunk, o, y).start()

        @pl.when(z + d < levels)
        def _():
            o = z + d
            landed(chunk, slot(o, y, c))

            @pl.when(bottom)
            def _():
                down(chunk, o).start()

            cross(chunk, o).start()
            core(chunk, o, y).start()

    def across(chunk, d):
        @pl.when(z - d >= 0)
        def _():
            landed(chunk, slot(z - d, 1 - y, c))
            core(chunk, z - d, 1 - y).start()

        if d > 0:

            @pl.when(z + d < levels)
            def _():
                landed(chunk, slot(z + d, 1 - y, c))
                core(chunk, z + d, 1 - y).start()

    def events(chunk):
        for d in range(1, levels):
            yield functools.partial(along, chunk, d)
            yield functools.partial(across, chunk, d - 1)
        yield functools.partial(across, chunk, levels - 1)

    pending = [list(events(chunk)) for chunk in range(4)]

    def advance(chunk, steps=None):
        steps = len(pending[chunk]) if steps is None else min(steps, len(pending[chunk]))
        for _ in range(steps):
            pending[chunk].pop(0)()

    def gathered(chunk):
        for o in range(levels):
            for yy in range(2):
                landed(chunk, slot(o, yy, 1 - c))

    def drain(chunk):
        for o in range(levels):

            @pl.when(top & (z >= o))
            def _():
                up(chunk, o).wait_send()

            @pl.when(bottom & (z <= o))
            def _():
                down(chunk, o).wait_send()

            cross(chunk, o).wait_send()
            for yy in range(2):
                core(chunk, o, yy).wait_send()

    half = tokens // 2

    def feature(i):
        rows = pl.ds(i * half, half)
        return remote(normed.at[rows], other.at[rows], feat_send.at[i], feat_recv.at[i], to_peer)

    own(0)
    feature(0).start()
    feature(1).start()
    mine_rows = pl.ds(pl.multiple_of(part * width, width), width)
    peer_rows = pl.ds(pl.multiple_of(peer * width, width), width)

    tall = (tokens, cap)
    query_hot = (lax.broadcasted_iota(jnp.int32, tall, 0) == query_row[...]).astype(BF16)
    key_hot = (lax.broadcasted_iota(jnp.int32, tall, 0) == key_row[...]).astype(BF16)
    inputs[0, :, mine_rows] = dot_tn(query_hot, normed[...]).astype(BF16)
    inputs[1, :, mine_rows] = dot_tn(key_hot, normed[...]).astype(BF16)
    load_qkv.wait()
    for j in range(3):
        share[j] = dot(normed[...], wide[j, mine_rows, :])
    def project(i):
        feature(i).wait_recv()
        rows = pl.ds(i * half, half)
        for j in range(3):
            value = share[j, rows, :] + dot(other[rows, :], wide[j, peer_rows, :])
            if j == 0:
                queries[rows, :] = value.astype(BF16)
            else:
                window[pl.ds(RADIUS + i * half, half), pl.ds((j - 1) * size, size)] = value.astype(
                    BF16
                )

    advance(0, 2)
    own(1)
    advance(0, 2)
    project(0)
    advance(0, 1)
    own(3)
    advance(0, 1)
    advance(1, 2)
    project(1)

    edge = pl.ds(RADIUS, RADIUS)
    last = pl.ds(tokens, RADIUS)
    halos = [
        remote(
            window.at[edge],
            window.at[pl.ds(tokens + RADIUS, RADIUS)],
            halo_send.at[0],
            halo_recv.at[0],
            {"seq": left},
        ),
        remote(
            window.at[last],
            window.at[pl.ds(0, RADIUS)],
            halo_send.at[1],
            halo_recv.at[1],
            {"seq": right},
        ),
    ]
    for halo in halos:
        halo.start()

    inputs[0, :, peer_rows] = dot_tn(query_hot, other[...]).astype(BF16)
    inputs[1, :, peer_rows] = dot_tn(key_hot, other[...]).astype(BF16)
    advance(0)
    advance(1, 2)
    gathered(0)
    slots = pl.ds(pl.multiple_of(me * cap, cap), cap)
    heavy_kv[slots, pl.ds(0, size)] = dot(inputs[1], pool[0]).astype(BF16)
    heavy_kv[slots, pl.ds(size, size)] = dot(inputs[1], pool[1]).astype(BF16)
    heavy_kv[slots, pl.ds(2 * size, BLOCK)] = (
        lax.broadcasted_iota(jnp.int32, (cap, BLOCK), 0) < key_count[...]
    ).astype(BF16)
    own(2)
    advance(1)
    advance(3, 2)
    load_out.wait()
    blocks = tokens // BLOCK

    def outgoing(r):
        rows = pl.ds(pl.multiple_of(r * BLOCK, BLOCK), BLOCK)
        return remote(away.at[rows], arrived.at[rows], out_send.at[r], out_recv.at[r], to_peer)

    def block(r):
        rows = pl.ds(pl.multiple_of(r * BLOCK, BLOCK), BLOCK)
        reach = pl.ds(pl.multiple_of(r * BLOCK, BLOCK), BLOCK + 2 * RADIUS)
        shape = (2 * BLOCK, BLOCK + 2 * RADIUS)
        row = lax.broadcasted_iota(jnp.int32, shape, 0)
        row = jnp.where(row < BLOCK, row, row - BLOCK)
        column = lax.broadcasted_iota(jnp.int32, shape, 1)
        gap = column - row
        place = me * tokens + r * BLOCK - RADIUS + column
        allowed = (gap >= 0) & (gap <= 2 * RADIUS) & (place >= 0) & (place < count * tokens)
        for h in range(size // PAIR):
            lanes = pl.ds(h * PAIR, PAIR)
            context[rows, lanes] = attend(
                queries[rows, lanes],
                window[reach, lanes],
                window[reach, pl.ds(size + h * PAIR, PAIR)],
                allowed,
                scale,
            )
        away[rows, :] = dot(context[rows, :], narrow[:, peer_rows]).astype(BF16)
        outgoing(r).start()

    for r in range(1, blocks - 1):
        block(r)
        advance(2, 2)
        advance(3, 2)
    for halo in halos:
        halo.wait_recv()
    block(0)
    advance(2)
    advance(3)
    block(blocks - 1)
    pieces = width // size
    for j in range(pieces):
        columns = pl.ds(pl.multiple_of(part * width + j * size, BLOCK), size)
        share[j] = dot(context[...], narrow[:, columns])
    gathered(1)
    heavy_q = dot(inputs[0], pool[2]).astype(BF16)
    logit = jnp.sum(
        inputs[0].astype(F32) * router[...].astype(F32)[None, :], axis=1, keepdims=True
    )
    gate = 1.0 / (1.0 + jnp.exp(-logit))
    live_slot = lax.broadcasted_iota(jnp.int32, (cap, 1), 0) < query_count[...]
    gate = jnp.where(live_slot, gate, 0.0)
    gathered(2)
    first = (lax.broadcasted_iota(jnp.int32, (2 * cap, BLOCK), 1) == 0).astype(BF16)
    live = dot_nt(first, heavy_kv[:, pl.ds(2 * size, BLOCK)]) > 0.5
    heavy_context = jnp.concatenate(
        [
            attend(
                heavy_q[:, h * PAIR : (h + 1) * PAIR],
                heavy_kv[:, pl.ds(h * PAIR, PAIR)],
                heavy_kv[:, pl.ds(size + h * PAIR, PAIR)],
                live,
                scale,
            )
            for h in range(size // PAIR)
        ],
        axis=1,
    )
    gathered(3)
    rows_away[...] = dot_nt(heavy_context, pool[3, peer_rows, :]) * gate
    row_copy = remote(rows_away, rows_in, row_send.at[0], row_recv.at[0], to_peer)
    row_copy.start()
    rows_mine = dot_nt(heavy_context, pool[3, mine_rows, :]) * gate
    row_copy.wait_recv()
    routed = (rows_mine + rows_in[...]).astype(BF16)
    for r in [*range(1, blocks - 1), 0, blocks - 1]:
        outgoing(r).wait_recv()
        rows = pl.ds(r * BLOCK, BLOCK)
        for j in range(pieces):
            columns = pl.ds(j * size, size)
            added = dot(query_hot[r * BLOCK : (r + 1) * BLOCK], routed[:, j * size : (j + 1) * size])
            result[rows, columns] = (
                share[j, rows, :] + arrived[rows, columns].astype(F32) + added
            ).astype(BF16)

    for chunk in range(4):
        drain(chunk)
    for i in range(2):
        feature(i).wait_send()
        halos[i].wait_send()
    for r in range(blocks):
        outgoing(r).wait_send()
    row_copy.wait_send()


def shards(
    count,
    normed,
    router,
    light_qkv,
    light_out,
    heavy_qkv,
    heavy_out,
    query_slots,
    query_count,
    key_slots,
    key_count,
):
    tokens, width = normed.shape
    size = light_out.shape[0]
    model = router.shape[0]
    cap = query_slots.shape[1]
    levels = count // 4
    vmem = pl.BlockSpec(memory_space=pltpu.VMEM)
    anywhere = pl.BlockSpec(memory_space=pl.ANY)
    blocks = tokens // BLOCK
    dma = pltpu.SemaphoreType.DMA
    return pl.pallas_call(
        functools.partial(kernel, count),
        out_shape=jax.ShapeDtypeStruct((tokens, width), BF16),
        in_specs=[vmem, vmem, anywhere, anywhere] + [vmem] * 6,
        out_specs=vmem,
        scratch_shapes=[
            pltpu.VMEM((tokens, width), BF16),
            pltpu.VMEM(light_qkv.shape, BF16),
            pltpu.VMEM(light_out.shape, BF16),
            pltpu.VMEM((4, model, size), BF16),
            pltpu.VMEM((3, tokens, size), F32),
            pltpu.VMEM((tokens, size), BF16),
            pltpu.VMEM((tokens + 2 * RADIUS, 2 * size), BF16),
            pltpu.VMEM((tokens, size), BF16),
            pltpu.VMEM((tokens, width), BF16),
            pltpu.VMEM((tokens, width), BF16),
            pltpu.VMEM((2, cap, model), BF16),
            pltpu.VMEM((count * cap, 2 * size + BLOCK), BF16),
            pltpu.VMEM((cap, width), F32),
            pltpu.VMEM((cap, width), F32),
            dma((2,)),
            dma((4, count)),
            dma((4, levels)),
            dma((4, levels)),
            dma((4, levels)),
            dma((4, 2 * levels)),
            dma((2,)),
            dma((2,)),
            dma((2,)),
            dma((2,)),
            dma((blocks,)),
            dma((blocks,)),
            dma((1,)),
            dma((1,)),
        ],
        compiler_params=pltpu.CompilerParams(
            collective_id=0, has_side_effects=True, vmem_limit_bytes=52 * 1024 * 1024
        ),
    )(
        normed,
        router,
        light_qkv,
        light_out,
        heavy_qkv,
        heavy_out,
        query_slots,
        key_slots,
        query_count[None],
        key_count[None],
    )


def solution(mesh):
    in_specs = (
        P("seq", "mp"),
        P(),
        P(None, None, "mp"),
        P("mp", None),
        P(None, "seq", "mp"),
        P("mp", "seq"),
        P("seq", None),
        P("seq"),
        P("seq", None),
        P("seq"),
    )
    return jax.shard_map(
        functools.partial(shards, mesh.shape["seq"]),
        mesh=mesh,
        in_specs=in_specs,
        out_specs=P("seq", "mp"),
        check_vma=False,
    )
```
